32 devices in a mesh: pole: 4 (over y, x), leaf: 8 (over z, core).
Axes of the slice: x: 2, y: 2, z: 4, core: 2. Of those that a mesh axis runs over, the one named last changes fastest.
Arguments:
- inverse_front: bfloat16 [4, 2, 8192, 8192], P('pole', None, 'leaf'), may hold values from -6 to 6
- factor_panel: bfloat16 [4, 8192, 512], P('pole', 'leaf'), may hold values from -0.0625 to 0.0625
- diag_inverse: bfloat16 [4, 256, 512], P('pole'), may hold values from -6 to 6
- pole_weight: float32 [4, 2], P('pole'), may hold values from -2.4 to 2.4
- structure: int32 [32], replicated, may hold values from 0 to 1, as said below
- block_owner: int32 [1024, 1], P('leaf'), may hold values from 0 to 7; in each aligned block of 128 rows (0 to 127, 128 to 255, ...) at most 32 rows name the same one
Outputs:
- owned_density: float32 [2048, 8, 256], P('leaf')
- diag_density: float32 [256, 256], replicated
The draws below stay inside these ranges and needn't reach their ends.
Inputs may be any that keep to these rules, and one draw needn't show every extreme that they name: `structure`: exactly 16 entries are 1. `block_owner`: among the 128 blocks of one index of leaf no owner appears more than 32 times, and in some index's blocks one owner appears exactly 32 times.
All inputs are finite; a program needn't handle non-finite values.
Results may differ from the reference program's by a relative error of at most 0.0003.
Values may be sent and summed in bfloat16 or wider, within the bound.
A program may use at most 128 MiB of HBM per device.

```python
import math
import jax
import jax.numpy as jnp
import numpy as np
from jax import lax

SN = 256
NF = 8192
RB = 8
POLES = 4
NBR = 32
NSEL = 16
NB = 1024
NB_DEV = 128
CAP = 32
SLOTS = 256
TOTAL_SLOTS = 2048
N_LEAF = 8


def draw_structure(key, part):
    order = jax.random.permutation(key, NBR).astype(jnp.int32)
    return (order < NSEL).astype(jnp.int32)


def level_of(rng, extent, pieces, smallest, high):
    loudness, own = 1.0, jax.random.fold_in(rng, 6)
    for axis_at, parts in pieces:
        steps = jnp.exp(jax.random.uniform(jax.random.fold_in(own, axis_at), (parts,), jnp.float32, smallest / len(pieces), high / len(pieces)))
        loudness = loudness * jnp.repeat(steps, extent[axis_at] // parts).reshape([-1 if axis == axis_at else 1 for axis in range(len(extent))])
    return loudness


def routed_block(rng, own, number, rows, number_of, top, reach, slope):
    ranking = jax.random.permutation(rng, number_of)
    heavy_load, usual = load_shares(number_of, rows * top, reach, slope, True), load_shares(number_of, rows * top, reach, slope, False)
    places = jnp.arange(number_of)

    def named(lengths, offset_by):
        used = int((lengths > 0).sum())
        fixed = max(1, used // 4)
        moved = fixed + (places - fixed + offset_by * (used - fixed)) % max(1, number_of - fixed)
        return jnp.zeros((number_of,), jnp.int32).at[ranking[jnp.where(places < fixed, places, moved)]].set(jnp.asarray(lengths, jnp.int32))

    lengths = jnp.where(number % 4 == 0, named(heavy_load, number // 4), named(usual, number - number // 4 - 1))
    mixed = jax.random.permutation(jax.random.fold_in(own, 3), number_of)
    source_of, taker = mixed[0:number_of // 2 * 2:2], mixed[1:number_of // 2 * 2:2]
    slack = jnp.minimum(lengths[source_of] - 1, reach - lengths[taker]) // 2
    slack = jnp.where((source_of == ranking[0]) | (taker == ranking[0]) | (lengths[taker] == 0), 0, jnp.maximum(slack, 0))
    moved = jax.random.randint(jax.random.fold_in(own, 4), (number_of // 2,), 0, 1 << 20) % (slack + 1)
    lengths = lengths.at[source_of].add(-moved).at[taker].add(moved)
    labels = jnp.searchsorted(jnp.cumsum(lengths), jnp.arange(rows * top), side="right").astype(jnp.int32)
    table = labels.reshape(top, rows).T
    table = table[jax.random.permutation(jax.random.fold_in(own, 1), rows)]
    offset_by = jax.random.randint(jax.random.fold_in(own, 2), (rows, 1), 0, top)
    return jnp.take_along_axis(table, (jnp.arange(top)[None, :] + offset_by) % top, axis=1)


def load_shares(amount, total, most, lean, full):
    weights = [(1 << 20) // math.isqrt(standing ** lean) + 1 for standing in range(1, amount + 1)]
    largest = most if full else min(most, max(-(-total // amount), total * weights[0] // sum(weights)))
    least = 1 if total - largest >= amount - 1 else 0
    counts, spare = [largest] + [least] * (amount - 1), total - largest - least * (amount - 1)
    while spare > 0:
        free = [i for i in range(1, amount) if counts[i] < largest] or [i for i in range(1, amount) if counts[i] < most]
        mass, budget = sum([weights[i] for i in free]), spare
        for i in free:
            extra = min(most - counts[i], max(1, budget * weights[i] // mass), spare)
            counts[i] = counts[i] + extra
            spare = spare - extra
    return np.array(counts)


def gaussian(stream_key, shape, scale, reach, pieces=(), kind=jnp.bfloat16):
    level = level_of(stream_key, shape, pieces, -0.22, 0.18) if pieces else 1.0
    entries = jax.random.normal(stream_key, shape, jnp.float32) * scale * level
    return jnp.minimum(jnp.maximum(entries, -reach), reach).astype(kind)


def setup_inputs(seed: int = 0) -> dict:
    seeds = jax.random.split(jax.random.key(seed), 7)
    inverse_front = gaussian(seeds[0], (POLES, 2, NF, NF), 1.0, 6.0, ((0, 4), (2, 8)))
    factor_panel = gaussian(seeds[1], (POLES, NF, 2 * SN), NF ** -0.5, 0.0625, ((0, 4), (1, 8)))
    diag_inverse = gaussian(seeds[2], (POLES, SN, 2 * SN), 1.0, 6.0, ((0, 4),))
    pole_weight = gaussian(seeds[3], (POLES, 2), 0.4, 2.4, ((0, 4),), jnp.float32)
    structure = draw_structure(jax.random.fold_in(seeds[6], 71), 0)
    block_owner_keys = jax.random.split(jax.random.fold_in(seeds[5], 1), NB // NB_DEV)
    block_owner_turns = jax.random.permutation(jax.random.fold_in(seeds[5], 3), NB // NB_DEV)
    block_owner = jax.vmap(lambda own, number: routed_block(jax.random.fold_in(seeds[5], 2), own, number, NB_DEV, N_LEAF, 1, CAP, 2))(block_owner_keys, block_owner_turns).reshape((NB, 1))
    return {"inverse_front": inverse_front, "factor_panel": factor_panel, "diag_inverse": diag_inverse, "pole_weight": pole_weight, "structure": structure, "block_owner": block_owner}


def chosen_rows(structure):
    order = jnp.argsort(1 - structure, stable=True)[:NSEL].astype(jnp.int32)
    return (order[:, None] * SN + jnp.arange(SN, dtype=jnp.int32)[None, :]).reshape(-1).astype(jnp.int32)


def reference(inverse_front, factor_panel, diag_inverse, pole_weight, structure, block_owner):
    precise = lax.Precision.HIGHEST
    selected = chosen_rows(structure)
    keep_rows = jnp.repeat(structure, SN).astype(jnp.float32)[:, None]

    def one_pole(carried, inputs):
        front_pole, panel_pole, diag_pole, weight_pole = inputs
        panel_used = jnp.take(panel_pole, selected, axis=0).astype(jnp.float32)
        column_real = jnp.take(front_pole[0], selected, axis=1).astype(jnp.float32)
        column_imag = jnp.take(front_pole[1], selected, axis=1).astype(jnp.float32)
        from_real = jnp.dot(column_real, panel_used, precision=precise)
        from_imag = jnp.dot(column_imag, panel_used, precision=precise)
        block_real = -(from_real[:, :SN] - from_imag[:, SN:]) * keep_rows
        block_imag = -(from_real[:, SN:] + from_imag[:, :SN]) * keep_rows
        panel_kept = panel_pole.astype(jnp.float32) * keep_rows
        panel_real = panel_kept[:, :SN]
        panel_imag = panel_kept[:, SN:]
        schur_real = jnp.dot(panel_real.T, block_real, precision=precise) - jnp.dot(panel_imag.T, block_imag, precision=precise)
        schur_imag = jnp.dot(panel_real.T, block_imag, precision=precise) + jnp.dot(panel_imag.T, block_real, precision=precise)
        diag_full = diag_pole.astype(jnp.float32)
        corner_real = diag_full[:, :SN] - schur_real
        corner_imag = diag_full[:, SN:] - schur_imag
        weight_real = weight_pole[0]
        weight_imag = weight_pole[1]
        density_rows = weight_real * block_imag + weight_imag * block_real
        density_corner = weight_real * corner_imag + weight_imag * corner_real
        return (carried[0] + density_rows, carried[1] + density_corner), None

    start_state = (jnp.zeros((NF, SN), jnp.float32), jnp.zeros((SN, SN), jnp.float32))
    (density, diag_density), _ = lax.scan(one_pole, start_state, (inverse_front, factor_panel, diag_inverse, pole_weight))

    blocks = density.reshape(NB, RB, SN)
    owners = block_owner[:, 0]
    sources = (jnp.arange(NB, dtype=jnp.int32) // NB_DEV).astype(jnp.int32)
    one_hot = (owners[:, None] == jnp.arange(N_LEAF, dtype=jnp.int32)[None, :]).astype(jnp.int32)
    grouped = one_hot.reshape(N_LEAF, NB_DEV, N_LEAF)
    earlier = (jnp.cumsum(grouped, axis=1) - grouped).reshape(NB, N_LEAF)
    ranks = jnp.sum(earlier * one_hot, axis=1).astype(jnp.int32)
    slot_index = (owners * SLOTS + sources * CAP + ranks).astype(jnp.int32)
    owned_density = jnp.zeros((TOTAL_SLOTS, RB, SN), jnp.float32).at[slot_index].set(blocks)
    return owned_density, diag_density
```

```python
import jax
import jax.numpy as jnp
from jax import lax
from jax.sharding import PartitionSpec as P


def body(inverse_front, factor_panel, diag_inverse, pole_weight, structure, block_owner):
    leaves = lax.axis_size("leaf")
    poles = lax.axis_size("pole")
    rows_here = inverse_front.shape[2]
    order = inverse_front.shape[3]
    width = factor_panel.shape[2] // 2
    rows_per = order // structure.shape[0]
    first_row = lax.axis_index("leaf") * rows_here
    panel = lax.all_gather(factor_panel[0], "leaf", axis=0, tiled=True)
    keep_all = jnp.repeat(structure, rows_per)
    keep_here = lax.dynamic_slice(keep_all, (first_row,), (rows_here,)).astype(jnp.float32)[:, None]
    masked = panel * keep_all.astype(jnp.bfloat16)[:, None]
    real = jnp.dot(inverse_front[0, 0], masked, preferred_element_type=jnp.float32)
    imag = jnp.dot(inverse_front[0, 1], masked, preferred_element_type=jnp.float32)
    block_real = -(real[:, :width] - imag[:, width:]) * keep_here
    block_imag = -(real[:, width:] + imag[:, :width]) * keep_here
    wr = pole_weight[0, 0]
    wi = pole_weight[0, 1]
    im_part = wr * block_imag + wi * block_real
    re_part = wr * block_real - wi * block_imag
    both = jnp.concatenate([im_part, re_part], axis=0)
    left = jnp.concatenate([factor_panel[0, :, :width], factor_panel[0, :, width:]], axis=0)
    rounded = lax.reduce_precision(both, 8, 7)
    high = rounded.astype(jnp.bfloat16)
    low = (both - rounded).astype(jnp.bfloat16)
    contract = (((0,), (0,)), ((), ()))
    corner = lax.dot_general(left, high, contract, preferred_element_type=jnp.float32)
    corner += lax.dot_general(left, low, contract, preferred_element_type=jnp.float32)
    diag = diag_inverse[0].astype(jnp.float32)
    diag = wr * diag[:, width:] + wi * diag[:, :width]
    diag = jnp.where(lax.axis_index("leaf") == 0, diag, 0.0)
    diag_density = lax.psum(diag - corner, ("pole", "leaf"))

    blocks = block_owner.shape[0]
    element_rows = rows_here // blocks
    capacity = max(2, (2 * blocks + leaves - 1) // leaves)
    piece = element_rows // poles * width
    pieces = im_part.reshape(blocks, poles, piece).transpose(1, 0, 2)
    mine = lax.psum_scatter(pieces, "pole", scatter_dimension=0, tiled=True)[0]
    owners = block_owner[:, 0]
    at = jnp.arange(blocks, dtype=jnp.int32)
    earlier = (owners[None, :] == owners[:, None]) & (at[None, :] < at[:, None])
    slot = owners * capacity + jnp.sum(earlier.astype(jnp.int32), axis=1)
    sent = jnp.zeros((leaves * capacity, piece), jnp.float32).at[slot].set(mine)
    got = lax.all_to_all(sent, "leaf", split_axis=0, concat_axis=0, tiled=True)
    full = lax.all_gather(got, "pole", axis=0)
    owned = full.transpose(1, 0, 2).reshape(leaves * capacity, element_rows, width)
    return owned, diag_density


def solution(mesh):
    placed = (
        P("pole", None, "leaf", None),
        P("pole", "leaf", None),
        P("pole", None, None),
        P("pole", None),
        P(),
        P("leaf", None),
    )
    return jax.shard_map(
        body, mesh=mesh, in_specs=placed, out_specs=(P("leaf", None, None), P()), check_vma=False
    )
```

```python
import functools
import jax
import jax.numpy as jnp
from jax import lax
from jax.experimental import pallas as pl
from jax.experimental.pallas import tpu as pltpu
from jax.sharding import PartitionSpec as P

CHUNKS = 1


def product_kernel(group, steps, kept, bands, rows_per, width, ids, weight, *refs):
    fronts = refs[:group]
    panels = refs[group : 2 * group]
    local, density, corner, total = refs[2 * group :]
    step = pl.program_id(0)
    transposed = (((0,), (0,)), ((), ()))

    @pl.when(step == 0)
    def _():
        corner[...] = jnp.zeros_like(corner)

    for band in range(bands):
        rows = pl.ds(band * rows_per, rows_per)
        used = ids[kept + band] == 1

        @pl.when(used)
        def _():
            for part in range(2):
                value = jnp.dot(fronts[0][0, part, rows], panels[0][...], preferred_element_type=jnp.float32)
                for g in range(1, group):
                    value += jnp.dot(fronts[g][0, part, rows], panels[g][...], preferred_element_type=jnp.float32)

                @pl.when(step == 0)
                def _():
                    total[part, rows] = value

                @pl.when(step > 0)
                def _():
                    total[part, rows] += value

        @pl.when(used & (step == steps - 1))
        def _():
            block_real = total[1, rows, width:] - total[0, rows, :width]
            block_imag = -(total[0, rows, width:] + total[1, rows, :width])
            wr = weight[0]
            wi = weight[1]
            im_part = wr * block_imag + wi * block_real
            re_part = wr * block_real - wi * block_imag
            density[rows] = im_part
            for left, right in ((local[0, rows, :width], im_part), (local[0, rows, width:], re_part)):
                high = right.astype(jnp.bfloat16)
                low = (right - high.astype(jnp.float32)).astype(jnp.bfloat16)
                corner[...] += lax.dot_general(left, high, transposed, preferred_element_type=jnp.float32)
                corner[...] += lax.dot_general(left, low, transposed, preferred_element_type=jnp.float32)

        @pl.when(jnp.logical_not(used) & (step == steps - 1))
        def _():
            density[rows] = jnp.zeros((rows_per, width), jnp.float32)


def product(ids, weight, front, panel, local, kept, rows_per):
    rows_here = front.shape[2]
    width = local.shape[2] // 2
    group = next(g for g in (4, 2, 1) if kept % g == 0)
    steps = kept // group
    bands = rows_here // rows_per

    def front_at(g, k, ids, weight):
        return (0, 0, 0, ids[k * group + g])

    def panel_at(g, k, ids, weight):
        return (ids[k * group + g], 0)

    in_specs = [
        pl.BlockSpec((1, 2, rows_here, rows_per), functools.partial(front_at, g)) for g in range(group)
    ]
    in_specs += [pl.BlockSpec((rows_per, 2 * width), functools.partial(panel_at, g)) for g in range(group)]
    in_specs.append(pl.BlockSpec((1, rows_here, 2 * width), lambda k, ids, weight: (0, 0, 0)))
    flops = 2 * 2 * rows_here * kept * rows_per * 2 * width
    return pl.pallas_call(
        functools.partial(product_kernel, group, steps, kept, bands, rows_per, width),
        out_shape=(
            jax.ShapeDtypeStruct((rows_here, width), jnp.float32),
            jax.ShapeDtypeStruct((width, width), jnp.float32),
        ),
        grid_spec=pltpu.PrefetchScalarGridSpec(
            num_scalar_prefetch=2,
            grid=(steps,),
            in_specs=in_specs,
            out_specs=(
                pl.BlockSpec((rows_here, width), lambda k, ids, weight: (0, 0)),
                pl.BlockSpec((width, width), lambda k, ids, weight: (0, 0)),
            ),
            scratch_shapes=[pltpu.VMEM((2, rows_here, 2 * width), jnp.float32)],
        ),
        compiler_params=pltpu.CompilerParams(vmem_limit_bytes=44 << 20),
        cost_estimate=pl.CostEstimate(
            flops=flops, bytes_accessed=4 * rows_here * kept * rows_per, transcendentals=0
        ),
    )(ids, weight, *([front] * group), *([panel] * group), local)


def body(inverse_front, factor_panel, diag_inverse, pole_weight, structure, block_owner):
    leaves = lax.axis_size("leaf")
    poles = lax.axis_size("pole")
    leaf = lax.axis_index("leaf")
    rows_here = inverse_front.shape[2]
    width = factor_panel.shape[2] // 2
    bands_all = structure.shape[0]
    rows_per = inverse_front.shape[3] // bands_all
    bands = rows_here // rows_per
    kept = bands_all // 2
    panel = lax.all_gather(factor_panel[0], "leaf", axis=0, tiled=True)

    band = jnp.arange(bands_all, dtype=jnp.int32)
    before = jnp.sum(jnp.where(band[None, :] < band[:, None], structure[None, :], 0), axis=1)
    hit = (before[None, :] == jnp.arange(kept, dtype=jnp.int32)[:, None]) & (structure[None, :] == 1)
    chosen = jnp.sum(jnp.where(hit, band[None, :], 0), axis=1)
    flags = lax.dynamic_slice(structure, (leaf * bands,), (bands,))
    ids = jnp.concatenate([chosen, flags]).astype(jnp.int32)
    density, corner = product(ids, pole_weight[0], inverse_front, panel, factor_panel, kept, rows_per)

    diag = diag_inverse[0].astype(jnp.float32)
    diag = pole_weight[0, 0] * diag[:, width:] + pole_weight[0, 1] * diag[:, :width]
    corner = jnp.where(leaf == 0, diag, 0.0) - corner

    blocks = block_owner.shape[0]
    element_rows = rows_here // blocks
    capacity = max(2, (2 * blocks + leaves - 1) // leaves)
    piece = element_rows // poles * width
    pieces = density.reshape(blocks, poles, piece).transpose(1, 0, 2)
    corners = corner.reshape(poles, -1, piece)
    owners = block_owner[:, 0]
    at = jnp.arange(blocks, dtype=jnp.int32)
    earlier = (owners[None, :] == owners[:, None]) & (at[None, :] < at[:, None])
    slot = owners * capacity + jnp.sum(earlier.astype(jnp.int32), axis=1)
    parts = []
    for chunk in range(CHUNKS):
        share = piece // CHUNKS
        some = pieces[:, :, chunk * share : (chunk + 1) * share]
        mine = lax.psum_scatter(some, "pole", scatter_dimension=0, tiled=True)[0]
        corner_some = corners[:, :, chunk * share : (chunk + 1) * share]
        corner_one = lax.psum_scatter(corner_some, "pole", scatter_dimension=0, tiled=True)
        corner_mine = jnp.sum(lax.all_gather(corner_one[0], "leaf", axis=0), axis=0)
        sent = jnp.zeros((leaves * capacity, share), jnp.float32).at[slot].set(mine)
        got = lax.all_to_all(sent, "leaf", split_axis=0, concat_axis=0, tiled=True)
        parts.append(lax.all_gather(jnp.concatenate([got, corner_mine], axis=0), "pole", axis=0))
    full = parts[0] if CHUNKS == 1 else jnp.concatenate(parts, axis=2)
    slots = leaves * capacity
    owned = full[:, :slots].transpose(1, 0, 2).reshape(slots, element_rows, width)
    return owned, full[:, slots:].reshape(width, width)


def solution(mesh):
    placed = (
        P("pole", None, "leaf", None),
        P("pole", "leaf", None),
        P("pole", None, None),
        P("pole", None),
        P(),
        P("leaf", None),
    )
    return jax.shard_map(
        body, mesh=mesh, in_specs=placed, out_specs=(P("leaf", None, None), P()), check_vma=False
    )
```

```python
import functools
import jax
import jax.numpy as jnp
from jax import lax
from jax.experimental import pallas as pl
from jax.experimental.pallas import tpu as pltpu
from jax.sharding import PartitionSpec as P

CHUNKS = 1


def product_kernel(group, steps, kept, bands, rows_per, width, ids, weight, *refs):
    fronts = refs[:group]
    panels = refs[group : 2 * group]
    local, density, corner, total = refs[2 * group :]
    step = pl.program_id(0)
    transposed = (((0,), (0,)), ((), ()))

    @pl.when(step == 0)
    def _():
        corner[...] = jnp.zeros_like(corner)

    for band in range(bands):
        rows = pl.ds(band * rows_per, rows_per)
        used = ids[kept + band] == 1

        @pl.when(used)
        def _():
            for part in range(2):
                value = jnp.dot(fronts[0][0, part, rows], panels[0][...], preferred_element_type=jnp.float32)
                for g in range(1, group):
                    value += jnp.dot(fronts[g][0, part, rows], panels[g][...], preferred_element_type=jnp.float32)

                @pl.when(step == 0)
                def _():
                    total[part, rows] = value

                @pl.when(step > 0)
                def _():
                    total[part, rows] += value

        @pl.when(used & (step == steps - 1))
        def _():
            block_real = total[1, rows, width:] - total[0, rows, :width]
            block_imag = -(total[0, rows, width:] + total[1, rows, :width])
            wr = weight[0]
            wi = weight[1]
            im_part = wr * block_imag + wi * block_real
            re_part = wr * block_real - wi * block_imag
            density[rows] = im_part
            for left, right in ((local[0, rows, :width], im_part), (local[0, rows, width:], re_part)):
                high = right.astype(jnp.bfloat16)
                low = (right - high.astype(jnp.float32)).astype(jnp.bfloat16)
                corner[...] += lax.dot_general(left, high, transposed, preferred_element_type=jnp.float32)
                corner[...] += lax.dot_general(left, low, transposed, preferred_element_type=jnp.float32)

        @pl.when(jnp.logical_not(used) & (step == steps - 1))
        def _():
            density[rows] = jnp.zeros((rows_per, width), jnp.float32)


def product(ids, weight, front, panel, local, kept, rows_per):
    rows_here = front.shape[2]
    width = local.shape[2] // 2
    group = next(g for g in (4, 2, 1) if kept % g == 0)
    steps = kept // group
    bands = rows_here // rows_per

    def front_at(g, k, ids, weight):
        return (0, 0, 0, ids[k * group + g])

    def panel_at(g, k, ids, weight):
        return (ids[k * group + g], 0)

    in_specs = [
        pl.BlockSpec((1, 2, rows_here, rows_per), functools.partial(front_at, g)) for g in range(group)
    ]
    in_specs += [pl.BlockSpec((rows_per, 2 * width), functools.partial(panel_at, g)) for g in range(group)]
    in_specs.append(pl.BlockSpec((1, rows_here, 2 * width), lambda k, ids, weight: (0, 0, 0)))
    flops = 2 * 2 * rows_here * kept * rows_per * 2 * width
    return pl.pallas_call(
        functools.partial(product_kernel, group, steps, kept, bands, rows_per, width),
        out_shape=(
            jax.ShapeDtypeStruct((rows_here, width), jnp.float32),
            jax.ShapeDtypeStruct((width, width), jnp.float32),
        ),
        grid_spec=pltpu.PrefetchScalarGridSpec(
            num_scalar_prefetch=2,
            grid=(steps,),
            in_specs=in_specs,
            out_specs=(
                pl.BlockSpec((rows_here, width), lambda k, ids, weight: (0, 0)),
                pl.BlockSpec((width, width), lambda k, ids, weight: (0, 0)),
            ),
            scratch_shapes=[pltpu.VMEM((2, rows_here, 2 * width), jnp.float32)],
        ),
        compiler_params=pltpu.CompilerParams(vmem_limit_bytes=44 << 20),
        cost_estimate=pl.CostEstimate(
            flops=flops, bytes_accessed=4 * rows_here * kept * rows_per, transcendentals=0
        ),
    )(ids, weight, *([front] * group), *([panel] * group), local)


def body(inverse_front, factor_panel, diag_inverse, pole_weight, structure, block_owner):
    leaves = lax.axis_size("leaf")
    poles = lax.axis_size("pole")
    leaf = lax.axis_index("leaf")
    rows_here = inverse_front.shape[2]
    width = factor_panel.shape[2] // 2
    bands_all = structure.shape[0]
    rows_per = inverse_front.shape[3] // bands_all
    bands = rows_here // rows_per
    kept = bands_all // 2
    panel = lax.all_gather(factor_panel[0], "leaf", axis=0, tiled=True)

    band = jnp.arange(bands_all, dtype=jnp.int32)
    before = jnp.sum(jnp.where(band[None, :] < band[:, None], structure[None, :], 0), axis=1)
    hit = (before[None, :] == jnp.arange(kept, dtype=jnp.int32)[:, None]) & (structure[None, :] == 1)
    chosen = jnp.sum(jnp.where(hit, band[None, :], 0), axis=1)
    flags = lax.dynamic_slice(structure, (leaf * bands,), (bands,))
    ids = jnp.concatenate([chosen, flags]).astype(jnp.int32)
    density, corner = product(ids, pole_weight[0], inverse_front, panel, factor_panel, kept, rows_per)

    diag = diag_inverse[0].astype(jnp.float32)
    diag = pole_weight[0, 0] * diag[:, width:] + pole_weight[0, 1] * diag[:, :width]
    corner = jnp.where(leaf == 0, diag, 0.0) - corner

    blocks = block_owner.shape[0]
    element_rows = rows_here // blocks
    capacity = max(2, (2 * blocks + leaves - 1) // leaves)
    piece = element_rows // poles * width
    pieces = density.reshape(blocks, poles, piece).transpose(1, 0, 2)
    pieces = jnp.concatenate([pieces, corner.reshape(poles, -1, piece)], axis=1)
    owners = block_owner[:, 0]
    at = jnp.arange(blocks, dtype=jnp.int32)
    earlier = (owners[None, :] == owners[:, None]) & (at[None, :] < at[:, None])
    slot = owners * capacity + jnp.sum(earlier.astype(jnp.int32), axis=1)
    parts = []
    for chunk in range(CHUNKS):
        share = piece // CHUNKS
        some = pieces[:, :, chunk * share : (chunk + 1) * share]
        mine = lax.psum_scatter(some.reshape(-1, share), "pole", scatter_dimension=0, tiled=True)
        corner_mine = jnp.sum(lax.all_gather(mine[blocks:], "leaf", axis=0), axis=0)
        sent = jnp.zeros((leaves * capacity, share), jnp.float32).at[slot].set(mine[:blocks])
        got = lax.all_to_all(sent, "leaf", split_axis=0, concat_axis=0, tiled=True)
        parts.append(lax.all_gather(jnp.concatenate([got, corner_mine], axis=0), "pole", axis=0))
    full = parts[0] if CHUNKS == 1 else jnp.concatenate(parts, axis=2)
    slots = leaves * capacity
    owned = full[:, :slots].transpose(1, 0, 2).reshape(slots, element_rows, width)
    return owned, full[:, slots:].reshape(width, width)


def solution(mesh):
    placed = (
        P("pole", None, "leaf", None),
        P("pole", "leaf", None),
        P("pole", None, None),
        P("pole", None),
        P(),
        P("leaf", None),
    )
    return jax.shard_map(
        body, mesh=mesh, in_specs=placed, out_specs=(P("leaf", None, None), P()), check_vma=False
    )
```
